128 devices in a mesh: tok: 4 (over x), exp: 32 (over y, z, core).
Axes of the slice: x: 4, y: 4, z: 4, core: 2. Of those that a mesh axis runs over, the one named last changes fastest.
Arguments:
- captured: bfloat16 [8192, 8, 1024], P(('tok', 'exp')), may hold values from -16 to 16
- expert_ids: int32 [8192, 8], P(('tok', 'exp')), may hold values from 0 to 127, all different within a row; in each aligned block of 32 rows (0 to 31, 32 to 63, ...) at most 4 rows name the same one
Outputs:
- whitening: float32 [128, 1024, 1024], P(('tok', 'exp'))
The draws below stay inside these ranges and needn't reach their ends.
Inputs may be any that keep to these rules, and one draw needn't show every extreme that they name: `expert_ids`: each row names 8 different experts; every expert is named by some row. In each aligned block of 32 token rows no expert is named more than 4 times, and in some block some expert is named exactly 4 times.
All inputs are finite; a program needn't handle non-finite values.
Results may differ from the reference program's by a relative error of at most 0.0003.
Values may be sent and summed in bfloat16 or wider, within the bound.
No kernel may reach another device: no remote copies, remote signals or barrier semaphores. Data moves between devices by JAX's collectives and lax.ppermute only.
A program may use at most 64 MiB of HBM per device.

```python
import math
import jax
import jax.numpy as jnp
import numpy as np
from jax import lax

H = 1024
TOP = 8
TOK_DEV = 64
EXPERTS = 128
TOKENS = 8192
MOST = 4


def draw_captured(key, part):
    subkeys = jax.random.split(key, 3)
    columns = jnp.exp(jax.random.uniform(subkeys[0], (H,), jnp.float32, math.log(0.3), math.log(3.0)))
    row_scale = jnp.exp(jax.random.uniform(subkeys[1], (TOKENS, TOP, 1), jnp.float32, math.log(0.5), math.log(2.0)))
    values = jax.random.normal(subkeys[2], (TOKENS, TOP, H), jnp.float32) * columns * row_scale
    return jnp.clip(values, -16.0, 16.0).astype(jnp.bfloat16)


def deal_out(own_key, own, number, rows, amount, top, limit, lean):
    order = jax.random.permutation(own_key, amount)
    packed, usual = load_shares(amount, rows * top, limit, lean, True), load_shares(amount, rows * top, limit, lean, False)
    places = jnp.arange(amount)

    def named(sizes, turn):
        used = int((sizes > 0).sum())
        fixed = max(1, used // 4)
        shifted = fixed + (places - fixed + turn * (used - fixed)) % max(1, amount - fixed)
        return jnp.zeros((amount,), jnp.int32).at[order[jnp.where(places < fixed, places, shifted)]].set(jnp.asarray(sizes, jnp.int32))

    sizes = jnp.where(number % 4 == 0, named(packed, number // 4), named(usual, number - number // 4 - 1))
    mixed = jax.random.permutation(jax.random.fold_in(own, 3), amount)
    donor, receiver = mixed[0:amount // 2 * 2:2], mixed[1:amount // 2 * 2:2]
    margin = jnp.minimum(sizes[donor] - 1, limit - sizes[receiver]) // 2
    margin = jnp.where((donor == order[0]) | (receiver == order[0]) | (sizes[receiver] == 0), 0, jnp.maximum(margin, 0))
    shifted = jax.random.randint(jax.random.fold_in(own, 4), (amount // 2,), 0, 1 << 20) % (margin + 1)
    sizes = sizes.at[donor].add(-shifted).at[receiver].add(shifted)
    items = jnp.searchsorted(jnp.cumsum(sizes), jnp.arange(rows * top), side="right").astype(jnp.int32)
    table = items.reshape(top, rows).T
    table = table[jax.random.permutation(jax.random.fold_in(own, 1), rows)]
    turn = jax.random.randint(jax.random.fold_in(own, 2), (rows, 1), 0, top)
    return jnp.take_along_axis(table, (jnp.arange(top)[None, :] + turn) % top, axis=1)


def load_shares(number_of, total, reach, skew, full):
    weights = [(1 << 20) // math.isqrt(grade ** skew) + 1 for grade in range(1, number_of + 1)]
    largest = reach if full else min(reach, max(-(-total // number_of), total * weights[0] // sum(weights)))
    least = 1 if total - largest >= number_of - 1 else 0
    given, rest = [largest] + [least] * (number_of - 1), total - largest - least * (number_of - 1)
    while rest > 0:
        movable = [i for i in range(1, number_of) if given[i] < largest] or [i for i in range(1, number_of) if given[i] < reach]
        mass, left = sum([weights[i] for i in movable]), rest
        for i in movable:
            addition = min(reach - given[i], max(1, left * weights[i] // mass), rest)
            given[i] = given[i] + addition
            rest = rest - addition
    return np.array(given)


def setup_inputs(seed: int = 0) -> dict:
    arg_keys = jax.random.split(jax.random.key(seed), 3)
    captured = draw_captured(jax.random.fold_in(arg_keys[2], 71), 0)
    expert_ids_keys = jax.random.split(jax.random.fold_in(arg_keys[1], 1), TOKENS // (TOK_DEV // 2))
    expert_ids_turns = jax.random.permutation(jax.random.fold_in(arg_keys[1], 3), TOKENS // (TOK_DEV // 2))
    expert_ids = jax.vmap(lambda own, number: deal_out(jax.random.fold_in(arg_keys[1], 2), own, number, TOK_DEV // 2, EXPERTS, TOP, MOST, 2))(expert_ids_keys, expert_ids_turns).reshape((TOKENS, TOP))
    return {"captured": captured, "expert_ids": expert_ids}


damping = 0.1

def whiten(gram, count):
    hess = gram / count
    shift = damping * jnp.mean(jnp.diagonal(hess))
    identity = jnp.eye(hess.shape[0], dtype=hess.dtype)
    hess = hess + shift * identity
    factor = jnp.linalg.cholesky(hess)
    return lax.linalg.triangular_solve(factor, identity, left_side=True, lower=True)

def reference(captured, expert_ids):
    flat_rows = captured.reshape(TOKENS * TOP, H)
    flat_ids = expert_ids.reshape(-1).astype(jnp.int32)
    expert_iota = jnp.arange(EXPERTS).astype(jnp.int32)
    counts_int = jnp.sum((flat_ids[:, None] == expert_iota[None, :]).astype(jnp.int32), axis=0).astype(jnp.int32)
    starts = (jnp.cumsum(counts_int) - counts_int).astype(jnp.int32)
    order = jnp.argsort(flat_ids, stable=True)
    capacity = EXPERTS * 2 * MOST
    ordered = jnp.concatenate([flat_rows[order], jnp.zeros((capacity, H), flat_rows.dtype)], axis=0)

    def one_expert(expert):
        start = starts[expert].astype(jnp.int32)
        count = counts_int[expert]
        block = lax.dynamic_slice_in_dim(ordered, start, capacity, 0)
        keep = jnp.arange(capacity).astype(jnp.int32) < count
        block = jnp.where(keep[:, None], block.astype(jnp.float32), jnp.float32(0.0))
        gram = lax.dot_general(block.astype(jnp.float32), block.astype(jnp.float32), (((0,), (0,)), ((), ())), precision=lax.Precision.HIGHEST, preferred_element_type=jnp.float32)
        return whiten(gram, count.astype(jnp.float32))
    return lax.map(one_expert, expert_iota)
```

```python
import jax
import jax.numpy as jnp
from jax import lax
from jax.experimental import pallas as pl
from jax.experimental.pallas import tpu as pltpu
from jax.sharding import PartitionSpec as P

damping = 0.1
EMPTY = 32.0
BLOCK = 128
PANEL = 8
F32 = jnp.float32
BF16 = jnp.bfloat16


def iota(shape, dim):
    return lax.broadcasted_iota(jnp.int32, shape, dim)


def route_kernel(slots_per_pair, ids_ref, rows_ref, out_ref, slot_ref):
    tokens, top = ids_ref.shape
    entries = tokens * top
    half = entries // 2
    tile = out_ref.shape[0]

    @pl.when(pl.program_id(0) == 0)
    def _():
        ids = ids_ref[...].astype(F32).astype(BF16)
        pick_col = (iota((entries, tokens), 0) // top == iota((entries, tokens), 1)).astype(F32).astype(BF16)
        by_col = jnp.dot(pick_col, ids, preferred_element_type=F32)
        keep = iota((entries, top), 0) % top == iota((entries, top), 1)
        id_col = jnp.sum(jnp.where(keep, by_col, 0.0), axis=1, keepdims=True)
        pick_row = (iota((tokens, entries), 1) // top == iota((tokens, entries), 0)).astype(F32).astype(BF16)
        by_row = lax.dot_general(ids, pick_row, (((0,), (0,)), ((), ())), preferred_element_type=F32)
        keep = iota((top, entries), 1) % top == iota((top, entries), 0)
        id_row = jnp.sum(jnp.where(keep, by_row, 0.0), axis=0, keepdims=True)
        earlier = iota((half, half), 0) < iota((half, half), 1)
        for part in range(2):
            col = id_col[part * half : (part + 1) * half]
            row = id_row[:, part * half : (part + 1) * half]
            rank = jnp.sum(jnp.where((col == row) & earlier, 1.0, 0.0), axis=0, keepdims=True)
            slot = row * slots_per_pair + rank + part * (slots_per_pair // 2)
            slot_ref[:, part * half : (part + 1) * half] = slot.astype(jnp.int32)

    first = pl.program_id(0) * tile
    onehot = jnp.where(iota((tile, entries), 0) + first == slot_ref[...], 1.0, 0.0)
    used = jnp.sum(onehot, axis=1, keepdims=True)
    moved = jnp.dot(onehot.astype(BF16), rows_ref[...], preferred_element_type=F32)
    mark = jnp.where(iota((tile, BLOCK), 1) == 0, EMPTY * (1.0 - used), 0.0)
    out_ref[:, :BLOCK] = (moved[:, :BLOCK] + mark).astype(BF16)
    out_ref[:, BLOCK:] = moved[:, BLOCK:].astype(BF16)


def route(captured, expert_ids, device_count):
    token_rows, top, width = captured.shape
    per_pair = token_rows * top * 2 // device_count
    slots = per_pair * device_count
    tile = 256
    return pl.pallas_call(
        lambda *refs: route_kernel(per_pair, *refs),
        grid=(slots // tile,),
        out_shape=jax.ShapeDtypeStruct((slots, width), BF16),
        in_specs=[
            pl.BlockSpec((token_rows, top), lambda i: (0, 0)),
            pl.BlockSpec((token_rows * top, width), lambda i: (0, 0)),
        ],
        out_specs=pl.BlockSpec((tile, width), lambda i: (i, 0)),
        scratch_shapes=[pltpu.VMEM((1, token_rows * top), jnp.int32)],
        compiler_params=pltpu.CompilerParams(vmem_limit_bytes=32 * 2**20),
        name="route",
    )(expert_ids, captured.reshape(token_rows * top, width))


LEFT = (0, 0, 1, 1, 0, 2)
RIGHT = (0, 1, 0, 1, 2, 0)


def pieces(x):
    first = x.astype(BF16)
    rest = x - first.astype(F32)
    second = rest.astype(BF16)
    third = (rest - second.astype(F32)).astype(BF16)
    return first, second, third


def left_stack(x):
    part = pieces(x)
    return jnp.concatenate([part[i] for i in LEFT], axis=1)


def right_stack(x, axis):
    part = pieces(x)
    return jnp.concatenate([part[i] for i in RIGHT], axis=axis)


def along_lanes(x, lane):
    return jnp.broadcast_to(x[:, lane : lane + 1], x.shape)


def along_sublanes(x, row):
    return jnp.broadcast_to(x[row : row + 1, :], x.shape)


def invert_factor(rows):
    lane = iota((PANEL, BLOCK), 1)
    sub = iota((PANEL, BLOCK), 0)
    rows = list(rows)
    count = len(rows)
    for p in range(count):
        base = p * PANEL
        corner = [along_lanes(rows[p], base + j) for j in range(PANEL)]
        below = {i: [along_lanes(rows[i], base + j) for j in range(PANEL)] for i in range(p + 1, count)}
        inside = (lane >= base) & (lane < base + PANEL)
        forward = jnp.where(inside, jnp.where(lane == sub + base, 1.0, 0.0), rows[p])
        full = forward
        pivots = jnp.ones_like(forward)
        inverses = jnp.ones_like(forward)
        for j in range(PANEL):
            pivot = along_sublanes(corner[j], j)
            inverse = 1.0 / pivot
            multiplier = jnp.where(sub == j, 0.0, corner[j] * inverse)
            for c in range(j + 1, PANEL):
                corner[c] = corner[c] - multiplier * along_sublanes(corner[c], j)
            row = along_sublanes(forward, j)
            forward = forward - jnp.where(sub > j, multiplier, 0.0) * row
            full = full - multiplier * row
            pivots = jnp.where(sub == j, pivot, pivots)
            inverses = jnp.where(sub == j, inverse, inverses)
        root = lax.rsqrt(pivots)
        root = root * (1.5 - 0.5 * pivots * root * root)
        rows[p] = forward * root
        full = full * inverses
        steps = [along_sublanes(full, j) for j in range(PANEL)]
        for i in range(p + 1, count):
            terms = [below[i][j] * steps[j] for j in range(PANEL)]
            while len(terms) > 1:
                terms = [a + b for a, b in zip(terms[::2], terms[1::2])]
            rows[i] = jnp.where(inside, 0.0, rows[i]) - terms[0]
    return rows


def whiten_kernel(x_ref, t_ref, right_ref):
    width = t_ref.shape[0]
    blocks = width // BLOCK
    contract_rows = (((0,), (0,)), ((), ()))
    contract_lanes = (((1,), (1,)), ((), ()))

    def gram_tile(i, _):
        at = pl.ds(pl.multiple_of(i * 2 * BLOCK, 2 * BLOCK), 2 * BLOCK)
        t_ref[at, :] = lax.dot_general(x_ref[:, at], x_ref[...], contract_rows, preferred_element_type=F32)
        return 0

    lax.fori_loop(0, blocks // 2, gram_tile, 0)

    lane = iota((x_ref.shape[0], BLOCK), 1)
    head = x_ref[:, :BLOCK].astype(F32)
    filled = (lane == 0) & (head != EMPTY)
    rows_here = jnp.sum(jnp.where(filled, 1.0, 0.0))
    square = jnp.sum(jnp.where(filled, head * head, 0.0))
    corner = t_ref[:PANEL, :BLOCK]
    at_origin = (iota((PANEL, BLOCK), 0) == 0) & (iota((PANEL, BLOCK), 1) == 0)
    t_ref[:PANEL, :BLOCK] = jnp.where(at_origin, square, corner)

    eye = iota((BLOCK, BLOCK), 0) == iota((BLOCK, BLOCK), 1)

    def block(i):
        return pl.ds(pl.multiple_of(i * BLOCK, BLOCK), BLOCK)

    diagonal = jnp.zeros((BLOCK, BLOCK), F32)
    for k in range(blocks):
        diagonal = diagonal + jnp.where(eye, t_ref[block(k), block(k)], 0.0)
    shift = damping * (jnp.sum(diagonal) / width)
    scale = jnp.sqrt(rows_here)
    lower = iota((BLOCK, BLOCK), 0) >= iota((BLOCK, BLOCK), 1)
    columns = iota((BLOCK, width), 1)

    def step(k, _):
        mine = block(k)
        spd = t_ref[mine, mine] + jnp.where(eye, shift, 0.0)
        done = invert_factor([spd[p * PANEL : (p + 1) * PANEL] for p in range(BLOCK // PANEL)])
        inverse = jnp.where(lower, jnp.concatenate(done, axis=0), 0.0)
        inverse_right = right_stack(inverse, 1)
        t_ref[mine, mine] = jnp.where(eye, 1.0, 0.0)
        solved = jnp.dot(left_stack(inverse), right_stack(t_ref[mine, :], 0), preferred_element_type=F32)
        right_ref[...] = right_stack(solved, 0)
        t_ref[mine, :] = jnp.where(columns < (k + 1) * BLOCK, solved * scale, 0.0)

        def update(i, _):
            panel = lax.dot_general(
                left_stack(t_ref[block(i), mine]), inverse_right, contract_lanes, preferred_element_type=F32
            )
            t_ref[block(i), mine] = jnp.zeros((BLOCK, BLOCK), F32)
            t_ref[block(i), :] -= jnp.dot(left_stack(panel), right_ref[...], preferred_element_type=F32)
            return 0

        lax.fori_loop(k + 1, blocks, update, 0)
        return 0

    lax.fori_loop(0, blocks, step, 0)


def whiten(arrived):
    width = arrived.shape[1]
    return pl.pallas_call(
        whiten_kernel,
        out_shape=jax.ShapeDtypeStruct((width, width), F32),
        in_specs=[pl.BlockSpec(memory_space=pltpu.VMEM)],
        out_specs=pl.BlockSpec(memory_space=pltpu.VMEM),
        scratch_shapes=[pltpu.VMEM((len(RIGHT) * BLOCK, width), BF16)],
        compiler_params=pltpu.CompilerParams(vmem_limit_bytes=40 * 2**20),
        name="whiten",
    )(arrived)


def shards(captured, expert_ids):
    device_count = lax.axis_size("tok") * lax.axis_size("exp")
    width = captured.shape[2]
    outbox = route(captured, expert_ids, device_count).reshape(device_count, -1, width)
    arrived = lax.all_to_all(outbox, ("tok", "exp"), split_axis=0, concat_axis=0, tiled=True)
    return whiten(arrived.reshape(-1, width))[None]


def solution(mesh):
    placed = (P(("tok", "exp"), None, None), P(("tok", "exp"), None))
    return jax.shard_map(
        shards, mesh=mesh, in_specs=placed, out_specs=P(("tok", "exp"), None, None), check_vma=False
    )
```

```python
import jax
import jax.numpy as jnp
from jax import lax
from jax.experimental import pallas as pl
from jax.experimental.pallas import tpu as pltpu
from jax.sharding import PartitionSpec as P

damping = 0.1
EMPTY = 32.0
BLOCK = 128
PANEL = 8
F32 = jnp.float32
BF16 = jnp.bfloat16


def iota(shape, dim):
    return lax.broadcasted_iota(jnp.int32, shape, dim)


def route_kernel(slots_per_pair, ids_ref, rows_ref, out_ref, slot_ref):
    tokens, top = ids_ref.shape
    entries = tokens * top
    half = entries // 2
    tile = out_ref.shape[0]

    @pl.when(pl.program_id(0) == 0)
    def _():
        ids = ids_ref[...].astype(F32).astype(BF16)
        pick_col = (iota((entries, tokens), 0) // top == iota((entries, tokens), 1)).astype(F32).astype(BF16)
        by_col = jnp.dot(pick_col, ids, preferred_element_type=F32)
        keep = iota((entries, top), 0) % top == iota((entries, top), 1)
        id_col = jnp.sum(jnp.where(keep, by_col, 0.0), axis=1, keepdims=True)
        pick_row = (iota((tokens, entries), 1) // top == iota((tokens, entries), 0)).astype(F32).astype(BF16)
        by_row = lax.dot_general(ids, pick_row, (((0,), (0,)), ((), ())), preferred_element_type=F32)
        keep = iota((top, entries), 1) % top == iota((top, entries), 0)
        id_row = jnp.sum(jnp.where(keep, by_row, 0.0), axis=0, keepdims=True)
        earlier = iota((half, half), 0) < iota((half, half), 1)
        for part in range(2):
            col = id_col[part * half : (part + 1) * half]
            row = id_row[:, part * half : (part + 1) * half]
            rank = jnp.sum(jnp.where((col == row) & earlier, 1.0, 0.0), axis=0, keepdims=True)
            slot = row * slots_per_pair + rank + part * (slots_per_pair // 2)
            slot_ref[:, part * half : (part + 1) * half] = slot.astype(jnp.int32)

    first = pl.program_id(0) * tile
    onehot = jnp.where(iota((tile, entries), 0) + first == slot_ref[...], 1.0, 0.0)
    used = jnp.sum(onehot, axis=1, keepdims=True)
    moved = jnp.dot(onehot.astype(BF16), rows_ref[...], preferred_element_type=F32)
    mark = jnp.where(iota((tile, BLOCK), 1) == 0, EMPTY * (1.0 - used), 0.0)
    out_ref[:, :BLOCK] = (moved[:, :BLOCK] + mark).astype(BF16)
    out_ref[:, BLOCK:] = moved[:, BLOCK:].astype(BF16)


def route(captured, expert_ids, device_count):
    token_rows, top, width = captured.shape
    per_pair = token_rows * top * 2 // device_count
    slots = per_pair * device_count
    tile = 256
    return pl.pallas_call(
        lambda *refs: route_kernel(per_pair, *refs),
        grid=(slots // tile,),
        out_shape=jax.ShapeDtypeStruct((slots, width), BF16),
        in_specs=[
            pl.BlockSpec((token_rows, top), lambda i: (0, 0)),
            pl.BlockSpec((token_rows * top, width), lambda i: (0, 0)),
        ],
        out_specs=pl.BlockSpec((tile, width), lambda i: (i, 0)),
        scratch_shapes=[pltpu.VMEM((1, token_rows * top), jnp.int32)],
        compiler_params=pltpu.CompilerParams(vmem_limit_bytes=32 * 2**20),
        name="route",
    )(expert_ids, captured.reshape(token_rows * top, width))


LEFT = (0, 0, 1, 1, 0, 2)
RIGHT = (0, 1, 0, 1, 2, 0)


def pieces(x):
    first = x.astype(BF16)
    rest = x - first.astype(F32)
    second = rest.astype(BF16)
    third = (rest - second.astype(F32)).astype(BF16)
    return first, second, third


def left_stack(x):
    part = pieces(x)
    return jnp.concatenate([part[i] for i in LEFT], axis=1)


def right_stack(x, axis):
    part = pieces(x)
    return jnp.concatenate([part[i] for i in RIGHT], axis=axis)


def along_lanes(x, lane):
    return jnp.broadcast_to(x[:, lane : lane + 1], x.shape)


def along_sublanes(x, row):
    return jnp.broadcast_to(x[row : row + 1, :], x.shape)


def add_up(terms):
    while len(terms) > 1:
        terms = [a + b for a, b in zip(terms[::2], terms[1::2])]
    return terms[0]


def invert_factor(rows, beside=lambda p: None):
    lane = iota((PANEL, BLOCK), 1)
    sub = iota((PANEL, BLOCK), 0)
    count = len(rows)
    each = range(PANEL)
    corner = [along_lanes(rows[0], j) for j in each]
    for p in range(count):
        base = p * PANEL
        more = p + 1 < count
        if more:
            beyond = [along_lanes(rows[p], base + PANEL + j) for j in each]
            corner_next = [along_lanes(rows[p + 1], base + PANEL + j) for j in each]
        below = {i: [along_lanes(rows[i], base + j) for j in each] for i in range(p + 1, count)}
        inside = (lane >= base) & (lane < base + PANEL)
        full = jnp.where(inside, jnp.where(lane == sub + base, 1.0, 0.0), rows[p])
        result = full
        for j in range(0, PANEL, 2):
            one, two = sub == j, sub == j + 1
            both = one | two
            a, b, c = (along_sublanes(corner[q], r) for q, r in ((j, j), (j + 1, j), (j + 1, j + 1)))
            det = a * c - b * b
            over = 1.0 / det
            left = jnp.where(one, -1.0, jnp.where(two, 0.0, corner[j]))
            right = jnp.where(two, -1.0, jnp.where(one, 0.0, corner[j + 1]))
            left_over = (left * c - right * b) * over
            right_over = (right * a - left * b) * over

            def sweep(x, soon):
                u, v = along_sublanes(x, j), along_sublanes(x, j + 1)
                kept = jnp.where(both, 0.0, x)
                if soon:
                    return kept - (left * (c * u - b * v) + right * (a * v - b * u)) * over
                return kept - (left_over * u + right_over * v)

            for q in each:
                if q not in (j, j + 1):
                    corner[q] = sweep(corner[q], q in (j + 2, j + 3))
            corner[j], corner[j + 1] = -left_over, -right_over
            u, v = along_sublanes(full, j), along_sublanes(full, j + 1)
            second = (a * v - b * u) * lax.rsqrt(a * det)
            result = jnp.where(one, u * lax.rsqrt(a), jnp.where(two, second, result))
            full = sweep(full, False)
        rows[p] = result
        if more:
            mixed = [add_up([below[p + 1][j] * along_sublanes(corner[q], j) for j in each]) for q in each]
            corner = [
                corner_next[q] - add_up([mixed[j] * along_sublanes(beyond[q], j) for j in each]) for q in each
            ]
        steps = [along_sublanes(full, j) for j in each]
        for i in range(p + 1, count):
            rows[i] = jnp.where(inside, 0.0, rows[i]) - add_up([below[i][j] * steps[j] for j in each])
        beside(p)


def whiten_kernel(x_ref, t_ref, left_ref, right_ref):
    width = t_ref.shape[0]
    blocks = width // BLOCK
    panels = BLOCK // PANEL
    contract_rows = (((0,), (0,)), ((), ()))
    contract_lanes = (((1,), (1,)), ((), ()))

    def gram_tile(i, _):
        at = pl.ds(pl.multiple_of(i * 2 * BLOCK, 2 * BLOCK), 2 * BLOCK)
        t_ref[at, :] = lax.dot_general(x_ref[:, at], x_ref[...], contract_rows, preferred_element_type=F32)
        return 0

    lax.fori_loop(0, blocks // 2, gram_tile, 0)

    lane = iota((x_ref.shape[0], BLOCK), 1)
    head = x_ref[:, :BLOCK].astype(F32)
    filled = (lane == 0) & (head != EMPTY)
    rows_here = jnp.sum(jnp.where(filled, 1.0, 0.0))
    square = jnp.sum(jnp.where(filled, head * head, 0.0))
    corner = t_ref[:PANEL, :BLOCK]
    at_origin = (iota((PANEL, BLOCK), 0) == 0) & (iota((PANEL, BLOCK), 1) == 0)
    t_ref[:PANEL, :BLOCK] = jnp.where(at_origin, square, corner)

    def at(k, stop=None):
        return slice(k * BLOCK, (k + 1 if stop is None else stop) * BLOCK)

    eye = iota((BLOCK, BLOCK), 0) == iota((BLOCK, BLOCK), 1)
    lower = iota((BLOCK, BLOCK), 0) >= iota((BLOCK, BLOCK), 1)
    diagonal = jnp.zeros((BLOCK, BLOCK), F32)
    for k in range(blocks):
        diagonal = diagonal + jnp.where(eye, t_ref[at(k), at(k)], 0.0)
    mean = jnp.sum(diagonal) / width
    unit = 1.0 / mean
    scale = jnp.sqrt(rows_here / mean)

    def read(rows, columns, k):
        return t_ref[rows, columns] * unit if k == 0 else t_ref[rows, columns]

    def damped(block):
        return block + jnp.where(eye, damping, 0.0)

    spd = damped(read(at(0), at(0), 0))
    pending = []

    def beside(p):
        for _ in range(-(-len(pending) // (panels - p))):
            pending.pop(0)()

    for k in range(blocks):
        rows = [spd[p * PANEL : (p + 1) * PANEL] for p in range(panels)]
        invert_factor(rows, beside)
        inverse = jnp.where(lower, jnp.concatenate(rows, axis=0), 0.0)
        inverse_left = left_stack(inverse)
        inverse_right = right_stack(inverse, 1)
        if k + 1 < blocks:
            across = jnp.dot(
                inverse_left, right_stack(read(at(k), at(k + 1), k), 0), preferred_element_type=F32
            )
            down = lax.dot_general(
                left_stack(read(at(k + 1), at(k), k)), inverse_right, contract_lanes, preferred_element_type=F32
            )
            spd = read(at(k + 1), at(k + 1), k)
            if k == 0:
                spd = damped(spd)
            spd = spd - jnp.dot(left_stack(down), right_stack(across, 0), preferred_element_type=F32)

        def solve(n, k=k, inverse=inverse, inverse_left=inverse_left):
            for m in (n, n + 1):
                if m == k:
                    right_ref[:, at(m)] = right_stack(inverse, 0)
                    t_ref[at(k), at(m)] = inverse * scale
            if n != k and n + 1 != k:
                parts = [(n, 2)]
            else:
                parts = [(n + 1 if n == k else n, 1)]
            for m, size in parts:
                columns = at(m, m + size)
                solved = jnp.dot(inverse_left, right_stack(read(at(k), columns, k), 0), preferred_element_type=F32)
                right_ref[:, columns] = right_stack(solved, 0)
                t_ref[at(k), columns] = solved * scale if m < k else jnp.zeros_like(solved)

        def descend(i, k=k, inverse_right=inverse_right):
            left_ref[at(i), :] = left_stack(
                lax.dot_general(
                    left_stack(read(at(i), at(k), k)), inverse_right, contract_lanes, preferred_element_type=F32
                )
            )
            t_ref[at(i), at(k)] = jnp.zeros((BLOCK, BLOCK), F32)

        def update(i, n, k=k):
            columns = at(n, n + 2)
            before = read(at(i), columns, k)
            if k == 0 and n <= i <= n + 1:
                places = iota(before.shape, 1) == iota(before.shape, 0) + (i - n) * BLOCK
                before = before + jnp.where(places, damping, 0.0)
            t_ref[at(i), columns] = before - jnp.dot(
                left_ref[at(i), :], right_ref[:, columns], preferred_element_type=F32
            )

        pending = [lambda n=n, solve=solve: solve(n) for n in range(0, blocks, 2)]
        pending += [lambda i=i, descend=descend: descend(i) for i in range(k + 1, blocks)]
        pending += [
            lambda i=i, n=n, update=update: update(i, n)
            for n in range(0, blocks, 2)
            for i in range(k + 1, blocks)
        ]
    while pending:
        pending.pop(0)()


def whiten(arrived):
    width = arrived.shape[1]
    return pl.pallas_call(
        whiten_kernel,
        out_shape=jax.ShapeDtypeStruct((width, width), F32),
        in_specs=[pl.BlockSpec(memory_space=pltpu.VMEM)],
        out_specs=pl.BlockSpec(memory_space=pltpu.VMEM),
        scratch_shapes=[
            pltpu.VMEM((width, len(LEFT) * BLOCK), BF16),
            pltpu.VMEM((len(RIGHT) * BLOCK, width), BF16),
        ],
        compiler_params=pltpu.CompilerParams(vmem_limit_bytes=40 * 2**20),
        name="whiten",
    )(arrived)


def shards(captured, expert_ids):
    device_count = lax.axis_size("tok") * lax.axis_size("exp")
    width = captured.shape[2]
    outbox = route(captured, expert_ids, device_count).reshape(device_count, -1, width)
    arrived = lax.all_to_all(outbox, ("tok", "exp"), split_axis=0, concat_axis=0, tiled=True)
    return whiten(arrived.reshape(-1, width))[None]


def solution(mesh):
    placed = (P(("tok", "exp"), None, None), P(("tok", "exp"), None))
    return jax.shard_map(
        shards, mesh=mesh, in_specs=placed, out_specs=P(("tok", "exp"), None, None), check_vma=False
    )
```

```python
import jax
import jax.numpy as jnp
from jax import lax
from jax.experimental import pallas as pl
from jax.experimental.pallas import tpu as pltpu
from jax.sharding import PartitionSpec as P

damping = 0.1
EMPTY = 32.0
BLOCK = 128
PANEL = 8
F32 = jnp.float32
BF16 = jnp.bfloat16


def iota(shape, dim):
    return lax.broadcasted_iota(jnp.int32, shape, dim)


def route_kernel(device_count, ids_ref, rows_hbm, out_ref, rows_ref, sem):
    fetch = pltpu.make_async_copy(rows_hbm, rows_ref, sem)
    fetch.start()
    top, tokens = ids_ref.shape
    entries = tokens * top
    half = entries // 2
    slots = out_ref.shape[0]
    per_pair = slots // device_count
    ids = ids_ref[...].astype(F32).astype(BF16)
    pick_col = (iota((entries, tokens), 0) // top == iota((entries, tokens), 1)).astype(F32).astype(BF16)
    by_col = lax.dot_general(pick_col, ids, (((1,), (1,)), ((), ())), preferred_element_type=F32)
    keep = iota((entries, top), 0) % top == iota((entries, top), 1)
    id_col = jnp.sum(jnp.where(keep, by_col, 0.0), axis=1, keepdims=True)
    pick_row = (iota((tokens, entries), 1) // top == iota((tokens, entries), 0)).astype(F32).astype(BF16)
    by_row = jnp.dot(ids, pick_row, preferred_element_type=F32)
    keep = iota((top, entries), 1) % top == iota((top, entries), 0)
    id_row = jnp.sum(jnp.where(keep, by_row, 0.0), axis=0, keepdims=True)
    earlier = iota((half, half), 0) < iota((half, half), 1)
    places = []
    for part in range(2):
        col = id_col[part * half : (part + 1) * half]
        row = id_row[:, part * half : (part + 1) * half]
        rank = jnp.sum(jnp.where((col == row) & earlier, 1.0, 0.0), axis=0, keepdims=True)
        places.append(row * per_pair + rank + part * (per_pair // 2))
    place = jnp.concatenate(places, axis=1).astype(jnp.int32)
    fetch.wait()
    tile = 2 * BLOCK
    for first in range(0, slots, tile):
        onehot = jnp.where(iota((tile, entries), 0) + first == place, 1.0, 0.0)
        used = jnp.sum(onehot, axis=1, keepdims=True)
        moved = jnp.dot(onehot.astype(BF16), rows_ref[...], preferred_element_type=F32)
        mark = jnp.where(iota((tile, BLOCK), 1) == 0, EMPTY * (1.0 - used), 0.0)
        out_ref[first : first + tile, :BLOCK] = (moved[:, :BLOCK] + mark).astype(BF16)
        out_ref[first : first + tile, BLOCK:] = moved[:, BLOCK:].astype(BF16)


def route(captured, expert_ids, device_count):
    token_rows, top, width = captured.shape
    slots = token_rows * top * 2
    return pl.pallas_call(
        lambda *refs: route_kernel(device_count, *refs),
        out_shape=jax.ShapeDtypeStruct((slots, width), BF16),
        in_specs=[pl.BlockSpec(memory_space=pltpu.VMEM), pl.BlockSpec(memory_space=pltpu.HBM)],
        out_specs=pl.BlockSpec(memory_space=pltpu.VMEM),
        scratch_shapes=[pltpu.VMEM((token_rows * top, width), BF16), pltpu.SemaphoreType.DMA(())],
        compiler_params=pltpu.CompilerParams(vmem_limit_bytes=32 * 2**20),
        name="route",
    )(expert_ids.T, captured.reshape(token_rows * top, width))


LEFT = (0, 0, 1, 1, 0, 2)
RIGHT = (0, 1, 0, 1, 2, 0)


def pieces(x):
    first = x.astype(BF16)
    rest = x - first.astype(F32)
    second = rest.astype(BF16)
    third = (rest - second.astype(F32)).astype(BF16)
    return first, second, third


def left_stack(x):
    part = pieces(x)
    return jnp.concatenate([part[i] for i in LEFT], axis=1)


def right_stack(x, axis):
    part = pieces(x)
    return jnp.concatenate([part[i] for i in RIGHT], axis=axis)


def along_lanes(x, lane):
    return jnp.broadcast_to(x[:, lane : lane + 1], x.shape)


def along_sublanes(x, row):
    return jnp.broadcast_to(x[row : row + 1, :], x.shape)


def add_up(terms):
    while len(terms) > 1:
        terms = [a + b for a, b in zip(terms[::2], terms[1::2])]
    return terms[0]


def invert_factor(rows, beside=lambda p: None):
    lane = iota((PANEL, BLOCK), 1)
    sub = iota((PANEL, BLOCK), 0)
    count = len(rows)
    each = range(PANEL)
    corner = [along_lanes(rows[0], j) for j in each]
    for p in range(count):
        base = p * PANEL
        more = p + 1 < count
        if more:
            beyond = [along_lanes(rows[p], base + PANEL + j) for j in each]
            corner_next = [along_lanes(rows[p + 1], base + PANEL + j) for j in each]
        below = {}

        def spread(i, base=base, below=below):
            below[i] = [along_lanes(rows[i], base + j) for j in each]

        far = list(range(p + 1, count))
        while far[:1] and far[0] <= p + 2:
            spread(far.pop(0))
        inside = (lane >= base) & (lane < base + PANEL)
        full = jnp.where(inside, jnp.where(lane == sub + base, 1.0, 0.0), rows[p])
        result = full
        for j in range(0, PANEL, 2):
            for _ in range(-(-len(far) // ((PANEL - j) // 2))):
                spread(far.pop(0))
            one, two = sub == j, sub == j + 1
            both = one | two
            a, b, c = (along_sublanes(corner[q], r) for q, r in ((j, j), (j + 1, j), (j + 1, j + 1)))
            det = a * c - b * b
            over = 1.0 / det
            left = jnp.where(one, -1.0, jnp.where(two, 0.0, corner[j]))
            right = jnp.where(two, -1.0, jnp.where(one, 0.0, corner[j + 1]))
            left_over = (left * c - right * b) * over
            right_over = (right * a - left * b) * over

            def sweep(x, soon):
                u, v = along_sublanes(x, j), along_sublanes(x, j + 1)
                kept = jnp.where(both, 0.0, x)
                if soon:
                    return kept - (left * (c * u - b * v) + right * (a * v - b * u)) * over
                return kept - (left_over * u + right_over * v)

            for q in each:
                if q not in (j, j + 1):
                    corner[q] = sweep(corner[q], q in (j + 2, j + 3))
            corner[j], corner[j + 1] = -left_over, -right_over
            u, v = along_sublanes(full, j), along_sublanes(full, j + 1)
            second = (a * v - b * u) * lax.rsqrt(a * det)
            result = jnp.where(one, u * lax.rsqrt(a), jnp.where(two, second, result))
            full = sweep(full, False)
        rows[p] = result
        if more:
            mixed = [add_up([below[p + 1][j] * along_sublanes(corner[q], j) for j in each]) for q in each]
            corner = [
                corner_next[q] - add_up([mixed[j] * along_sublanes(beyond[q], j) for j in each]) for q in each
            ]
        steps = [along_sublanes(full, j) for j in each]
        for i in range(p + 1, count):
            rows[i] = jnp.where(inside, 0.0, rows[i]) - add_up([below[i][j] * steps[j] for j in each])
        beside(p)


def whiten_kernel(x_ref, out_ref, t_ref, turned_ref, left_ref, right_ref, sems):
    total, width = x_ref.shape
    blocks = width // BLOCK
    panels = BLOCK // PANEL
    contract_lanes = (((1,), (1,)), ((), ()))

    def at(k, stop=None):
        return slice(k * BLOCK, (k + 1 if stop is None else stop) * BLOCK)

    first = iota((BLOCK, BLOCK), 1) == 0

    def squares(i, sums):
        filled, corner, trace = sums
        mine = pl.ds(pl.multiple_of(i * BLOCK, BLOCK), BLOCK)
        head = x_ref[mine, :BLOCK].astype(F32)
        real = first & (head != EMPTY)
        square = jnp.where(real, head * head, 0.0)
        filled = filled + jnp.where(real, 1.0, 0.0)
        corner = corner + square
        trace = trace + jnp.where(first, 0.0, head * head) + square
        for k in range(1, blocks):
            more = x_ref[mine, at(k)].astype(F32)
            trace = trace + more * more
        return filled, corner, trace

    sums = lax.fori_loop(0, total // BLOCK, squares, (jnp.zeros((BLOCK, BLOCK), F32),) * 3)
    rows_here, square, trace = (jnp.sum(part) for part in sums)

    eye = iota((BLOCK, BLOCK), 0) == iota((BLOCK, BLOCK), 1)
    lower = iota((BLOCK, BLOCK), 0) >= iota((BLOCK, BLOCK), 1)
    mean = trace / width
    unit = 1.0 / mean
    scale = jnp.sqrt(rows_here / mean)

    def turn(i):
        turned_ref[at(i), :] = x_ref[:, at(i)].T

    turn(0)
    spd = jnp.dot(turned_ref[at(0), :], x_ref[:, at(0)], preferred_element_type=F32)
    origin = eye & (iota((BLOCK, BLOCK), 0) == 0)
    spd = jnp.where(origin, square, spd) * unit + jnp.where(eye, damping, 0.0)

    def gram(i, n):
        mine, columns = at(i, i + 2), at(n, n + 2)
        block = jnp.dot(turned_ref[mine, :], x_ref[:, columns], preferred_element_type=F32) * unit
        if i == n:
            block = block + jnp.where(iota(block.shape, 0) == iota(block.shape, 1), damping, 0.0)
        t_ref[mine, columns] = block

    pending = [lambda i=i: turn(i) for i in range(1, blocks)]
    pending += [lambda i=i, n=n: gram(i, n) for i in range(0, blocks, 2) for n in range(0, blocks, 2)]
    sends = []

    def beside(p):
        for _ in range(-(-len(pending) // (panels - p))):
            pending.pop(0)()

    for k in range(blocks):
        rows = [spd[p * PANEL : (p + 1) * PANEL] for p in range(panels)]
        invert_factor(rows, beside)
        inverse = jnp.where(lower, jnp.concatenate(rows, axis=0), 0.0)
        inverse_left = left_stack(inverse)
        inverse_right = right_stack(inverse, 1)
        if k + 1 < blocks:
            across = jnp.dot(
                inverse_left, right_stack(t_ref[at(k), at(k + 1)], 0), preferred_element_type=F32
            )
            down = lax.dot_general(
                left_stack(t_ref[at(k + 1), at(k)]), inverse_right, contract_lanes, preferred_element_type=F32
            )
            spd = t_ref[at(k + 1), at(k + 1)] - jnp.dot(left_stack(down), right_stack(across, 0), preferred_element_type=F32)

        def solve(n, k=k, inverse=inverse, inverse_left=inverse_left):
            for m in (n, n + 1):
                if m == k:
                    right_ref[:, at(m)] = right_stack(inverse, 0)
                    t_ref[at(k), at(m)] = inverse * scale
            if n != k and n + 1 != k:
                parts = [(n, 2)]
            else:
                parts = [(n + 1 if n == k else n, 1)]
            for m, size in parts:
                columns = at(m, m + size)
                solved = jnp.dot(inverse_left, right_stack(t_ref[at(k), columns], 0), preferred_element_type=F32)
                right_ref[:, columns] = right_stack(solved, 0)
                t_ref[at(k), columns] = solved * scale if m < k else jnp.zeros_like(solved)

        def descend(i, k=k, inverse_right=inverse_right):
            left_ref[at(i), :] = left_stack(
                lax.dot_general(
                    left_stack(t_ref[at(i), at(k)]), inverse_right, contract_lanes, preferred_element_type=F32
                )
            )
            t_ref[at(i), at(k)] = jnp.zeros((BLOCK, BLOCK), F32)

        def update(i, n, k=k):
            columns = at(n, n + 2)
            t_ref[at(i), columns] -= jnp.dot(left_ref[at(i), :], right_ref[:, columns], preferred_element_type=F32)

        def send(k=k):
            sends.append(pltpu.make_async_copy(t_ref.at[at(k), :], out_ref.at[at(k), :], sems.at[k]))
            sends[-1].start()

        pending = [lambda n=n, solve=solve: solve(n) for n in range(0, blocks, 2)]
        pending += [send]
        pending += [lambda i=i, descend=descend: descend(i) for i in range(k + 1, blocks)]
        pending += [
            lambda i=i, n=n, update=update: update(i, n)
            for n in range(0, blocks, 2)
            for i in range(k + 1, blocks)
        ]
    while pending:
        pending.pop(0)()
    for copy in sends:
        copy.wait()


def whiten(arrived):
    width = arrived.shape[1]
    return pl.pallas_call(
        whiten_kernel,
        out_shape=jax.ShapeDtypeStruct((width, width), F32),
        in_specs=[pl.BlockSpec(memory_space=pltpu.VMEM)],
        out_specs=pl.BlockSpec(memory_space=pltpu.HBM),
        scratch_shapes=[
            pltpu.VMEM((width, width), F32),
            pltpu.VMEM((width, arrived.shape[0]), BF16),
            pltpu.VMEM((width, len(LEFT) * BLOCK), BF16),
            pltpu.VMEM((len(RIGHT) * BLOCK, width), BF16),
            pltpu.SemaphoreType.DMA((width // BLOCK,)),
        ],
        compiler_params=pltpu.CompilerParams(vmem_limit_bytes=40 * 2**20),
        name="whiten",
    )(arrived)


def shards(captured, expert_ids):
    device_count = lax.axis_size("tok") * lax.axis_size("exp")
    width = captured.shape[2]
    outbox = route(captured, expert_ids, device_count).reshape(device_count, -1, width)
    arrived = lax.all_to_all(outbox, ("tok", "exp"), split_axis=0, concat_axis=0, tiled=True)
    return whiten(arrived.reshape(-1, width))[None]


def solution(mesh):
    placed = (P(("tok", "exp"), None, None), P(("tok", "exp"), None))
    return jax.shard_map(
        shards, mesh=mesh, in_specs=placed, out_specs=P(("tok", "exp"), None, None), check_vma=False
    )
```

```python
import jax
import jax.numpy as jnp
from jax import lax
from jax.experimental import pallas as pl
from jax.experimental.pallas import tpu as pltpu
from jax.sharding import PartitionSpec as P

damping = 0.1
EMPTY = 32.0
BLOCK = 128
PANEL = 8
F32 = jnp.float32
BF16 = jnp.bfloat16


def iota(shape, dim):
    return lax.broadcasted_iota(jnp.int32, shape, dim)


def route_kernel(device_count, ids_ref, rows_hbm, out_ref, rows_ref, sem):
    fetch = pltpu.make_async_copy(rows_hbm, rows_ref, sem)
    fetch.start()
    top, tokens = ids_ref.shape
    entries = tokens * top
    half = entries // 2
    slots = out_ref.shape[0]
    per_pair = slots // device_count
    ids = ids_ref[...].astype(F32).astype(BF16)
    pick_col = (iota((entries, tokens), 0) // top == iota((entries, tokens), 1)).astype(F32).astype(BF16)
    by_col = lax.dot_general(pick_col, ids, (((1,), (1,)), ((), ())), preferred_element_type=F32)
    keep = iota((entries, top), 0) % top == iota((entries, top), 1)
    id_col = jnp.sum(jnp.where(keep, by_col, 0.0), axis=1, keepdims=True)
    pick_row = (iota((tokens, entries), 1) // top == iota((tokens, entries), 0)).astype(F32).astype(BF16)
    by_row = jnp.dot(ids, pick_row, preferred_element_type=F32)
    keep = iota((top, entries), 1) % top == iota((top, entries), 0)
    id_row = jnp.sum(jnp.where(keep, by_row, 0.0), axis=0, keepdims=True)
    earlier = iota((half, half), 0) < iota((half, half), 1)
    places = []
    for part in range(2):
        col = id_col[part * half : (part + 1) * half]
        row = id_row[:, part * half : (part + 1) * half]
        rank = jnp.sum(jnp.where((col == row) & earlier, 1.0, 0.0), axis=0, keepdims=True)
        places.append(row * per_pair + rank + part * (per_pair // 2))
    place = jnp.concatenate(places, axis=1).astype(jnp.int32)
    fetch.wait()
    tile = 2 * BLOCK
    for first in range(0, slots, tile):
        onehot = jnp.where(iota((tile, entries), 0) + first == place, 1.0, 0.0)
        used = jnp.sum(onehot, axis=1, keepdims=True)
        moved = jnp.dot(onehot.astype(BF16), rows_ref[...], preferred_element_type=F32)
        mark = jnp.where(iota((tile, BLOCK), 1) == 0, EMPTY * (1.0 - used), 0.0)
        out_ref[first : first + tile, :BLOCK] = (moved[:, :BLOCK] + mark).astype(BF16)
        out_ref[first : first + tile, BLOCK:] = moved[:, BLOCK:].astype(BF16)


def route(captured, expert_ids, device_count):
    token_rows, top, width = captured.shape
    slots = token_rows * top * 2
    return pl.pallas_call(
        lambda *refs: route_kernel(device_count, *refs),
        out_shape=jax.ShapeDtypeStruct((slots, width), BF16),
        in_specs=[pl.BlockSpec(memory_space=pltpu.VMEM), pl.BlockSpec(memory_space=pltpu.HBM)],
        out_specs=pl.BlockSpec(memory_space=pltpu.VMEM),
        scratch_shapes=[pltpu.VMEM((token_rows * top, width), BF16), pltpu.SemaphoreType.DMA(())],
        compiler_params=pltpu.CompilerParams(vmem_limit_bytes=32 * 2**20),
        name="route",
    )(expert_ids.T, captured.reshape(token_rows * top, width))


LEFT = (0, 0, 1, 1, 0, 2)
RIGHT = (0, 1, 0, 1, 2, 0)


def pieces(x):
    first = x.astype(BF16)
    rest = x - first.astype(F32)
    second = rest.astype(BF16)
    third = (rest - second.astype(F32)).astype(BF16)
    return first, second, third


def left_stack(x):
    part = pieces(x)
    return jnp.concatenate([part[i] for i in LEFT], axis=1)


def right_stack(x, axis):
    part = pieces(x)
    return jnp.concatenate([part[i] for i in RIGHT], axis=axis)


def along_lanes(x, lane):
    return jnp.take_along_axis(x, jnp.full(x.shape, lane, jnp.int32), axis=1, mode="promise_in_bounds")


def along_sublanes(x, row):
    return jnp.broadcast_to(x[row : row + 1, :], x.shape)


def add_up(terms):
    while len(terms) > 1:
        terms = [a + b for a, b in zip(terms[::2], terms[1::2])]
    return terms[0]


def invert_factor(rows, beside=lambda p: None):
    lane = iota((PANEL, BLOCK), 1)
    sub = iota((PANEL, BLOCK), 0)
    count = len(rows)
    each = range(PANEL)
    corner = [along_lanes(rows[0], j) for j in each]
    for p in range(count):
        base = p * PANEL
        more = p + 1 < count
        if more:
            beyond = [along_lanes(rows[p], base + PANEL + j) for j in each]
            corner_next = [along_lanes(rows[p + 1], base + PANEL + j) for j in each]
        below = {}

        def spread(i, base=base, below=below):
            below[i] = [along_lanes(rows[i], base + j) for j in each]

        far = list(range(p + 1, count))
        while far[:1] and far[0] <= p + 2:
            spread(far.pop(0))
        inside = (lane >= base) & (lane < base + PANEL)
        full = jnp.where(inside, jnp.where(lane == sub + base, 1.0, 0.0), rows[p])
        result = full
        for j in range(0, PANEL, 2):
            for _ in range(-(-len(far) // ((PANEL - j) // 2))):
                spread(far.pop(0))
            one, two = sub == j, sub == j + 1
            both = one | two
            a, b, c = (along_sublanes(corner[q], r) for q, r in ((j, j), (j + 1, j), (j + 1, j + 1)))
            det = a * c - b * b
            over = 1.0 / det
            left = jnp.where(one, -1.0, jnp.where(two, 0.0, corner[j]))
            right = jnp.where(two, -1.0, jnp.where(one, 0.0, corner[j + 1]))
            left_over = (left * c - right * b) * over
            right_over = (right * a - left * b) * over

            def sweep(x):
                u, v = along_sublanes(x, j), along_sublanes(x, j + 1)
                return jnp.where(both, 0.0, x) - (left_over * u + right_over * v)

            for q in each:
                if q not in (j, j + 1):
                    corner[q] = sweep(corner[q])
            corner[j], corner[j + 1] = -left_over, -right_over
            u, v = along_sublanes(full, j), along_sublanes(full, j + 1)
            second = (a * v - b * u) * lax.rsqrt(a * det)
            result = jnp.where(one, u * lax.rsqrt(a), jnp.where(two, second, result))
            full = sweep(full)
        rows[p] = result
        if more:
            mixed = [add_up([below[p + 1][j] * along_sublanes(corner[q], j) for j in each]) for q in each]
            corner = [
                corner_next[q] - add_up([mixed[j] * along_sublanes(beyond[q], j) for j in each]) for q in each
            ]
        steps = [along_sublanes(full, j) for j in each]
        for i in range(p + 1, count):
            rows[i] = jnp.where(inside, 0.0, rows[i]) - add_up([below[i][j] * steps[j] for j in each])
        beside(p)


def whiten_kernel(x_ref, out_ref, t_ref, turned_ref, left_ref, right_ref, sems):
    total, width = x_ref.shape
    blocks = width // BLOCK
    panels = BLOCK // PANEL
    contract_lanes = (((1,), (1,)), ((), ()))

    def at(k, stop=None):
        return slice(k * BLOCK, (k + 1 if stop is None else stop) * BLOCK)

    first = iota((BLOCK, BLOCK), 1) == 0

    def squares(i, sums):
        filled, corner, trace = sums
        mine = pl.ds(pl.multiple_of(i * BLOCK, BLOCK), BLOCK)
        head = x_ref[mine, :BLOCK].astype(F32)
        real = first & (head != EMPTY)
        square = jnp.where(real, head * head, 0.0)
        filled = filled + jnp.where(real, 1.0, 0.0)
        corner = corner + square
        trace = trace + jnp.where(first, 0.0, head * head) + square
        for k in range(1, blocks):
            more = x_ref[mine, at(k)].astype(F32)
            trace = trace + more * more
        return filled, corner, trace

    sums = lax.fori_loop(0, total // BLOCK, squares, (jnp.zeros((BLOCK, BLOCK), F32),) * 3)
    rows_here, square, trace = (jnp.sum(part) for part in sums)

    eye = iota((BLOCK, BLOCK), 0) == iota((BLOCK, BLOCK), 1)
    lower = iota((BLOCK, BLOCK), 0) >= iota((BLOCK, BLOCK), 1)
    mean = trace / width
    unit = 1.0 / mean
    scale = jnp.sqrt(rows_here / mean)

    def turn(i):
        turned_ref[at(i), :] = x_ref[:, at(i)].T

    turn(0)
    spd = jnp.dot(turned_ref[at(0), :], x_ref[:, at(0)], preferred_element_type=F32)
    origin = eye & (iota((BLOCK, BLOCK), 0) == 0)
    spd = jnp.where(origin, square, spd) * unit + jnp.where(eye, damping, 0.0)

    def gram(i, n):
        mine, columns = at(i, i + 2), at(n, n + 2)
        block = jnp.dot(turned_ref[mine, :], x_ref[:, columns], preferred_element_type=F32) * unit
        if i == n:
            block = block + jnp.where(iota(block.shape, 0) == iota(block.shape, 1), damping, 0.0)
        t_ref[mine, columns] = block

    pending = [lambda i=i: turn(i) for i in range(1, blocks)]
    pending += [lambda i=i, n=n: gram(i, n) for i in range(0, blocks, 2) for n in range(0, blocks, 2)]
    sends = []

    def beside(p):
        for _ in range(-(-len(pending) // (panels - p))):
            pending.pop(0)()

    for k in range(blocks):
        rows = [spd[p * PANEL : (p + 1) * PANEL] for p in range(panels)]
        invert_factor(rows, beside)
        inverse = jnp.where(lower, jnp.concatenate(rows, axis=0), 0.0)
        inverse_left = left_stack(inverse)
        inverse_right = right_stack(inverse, 1)
        if k + 1 < blocks:
            across = jnp.dot(
                inverse_left, right_stack(t_ref[at(k), at(k + 1)], 0), preferred_element_type=F32
            )
            down = lax.dot_general(
                left_stack(t_ref[at(k + 1), at(k)]), inverse_right, contract_lanes, preferred_element_type=F32
            )
            spd = t_ref[at(k + 1), at(k + 1)] - jnp.dot(left_stack(down), right_stack(across, 0), preferred_element_type=F32)

        def solve(n, k=k, inverse=inverse, inverse_left=inverse_left):
            for m in (n, n + 1):
                if m == k:
                    right_ref[:, at(m)] = right_stack(inverse, 0)
                    t_ref[at(k), at(m)] = inverse * scale
            if n != k and n + 1 != k:
                parts = [(n, 2)]
            else:
                parts = [(n + 1 if n == k else n, 1)]
            for m, size in parts:
                columns = at(m, m + size)
                solved = jnp.dot(inverse_left, right_stack(t_ref[at(k), columns], 0), preferred_element_type=F32)
                right_ref[:, columns] = right_stack(solved, 0)
                t_ref[at(k), columns] = solved * scale if m < k else jnp.zeros_like(solved)

        def descend(i, k=k, inverse_right=inverse_right):
            left_ref[at(i), :] = left_stack(
                lax.dot_general(
                    left_stack(t_ref[at(i), at(k)]), inverse_right, contract_lanes, preferred_element_type=F32
                )
            )
            t_ref[at(i), at(k)] = jnp.zeros((BLOCK, BLOCK), F32)

        def update(i, n, k=k):
            columns = at(n, n + 2)
            t_ref[at(i), columns] -= jnp.dot(left_ref[at(i), :], right_ref[:, columns], preferred_element_type=F32)

        def send(k=k):
            sends.append(pltpu.make_async_copy(t_ref.at[at(k), :], out_ref.at[at(k), :], sems.at[k]))
            sends[-1].start()

        pending = [lambda n=n, solve=solve: solve(n) for n in range(0, blocks, 2)]
        pending += [send]
        pending += [lambda i=i, descend=descend: descend(i) for i in range(k + 1, blocks)]
        pending += [
            lambda i=i, n=n, update=update: update(i, n)
            for n in range(0, blocks, 2)
            for i in range(k + 1, blocks)
        ]
    while pending:
        pending.pop(0)()
    for copy in sends:
        copy.wait()


def whiten(arrived):
    width = arrived.shape[1]
    return pl.pallas_call(
        whiten_kernel,
        out_shape=jax.ShapeDtypeStruct((width, width), F32),
        in_specs=[pl.BlockSpec(memory_space=pltpu.VMEM)],
        out_specs=pl.BlockSpec(memory_space=pltpu.HBM),
        scratch_shapes=[
            pltpu.VMEM((width, width), F32),
            pltpu.VMEM((width, arrived.shape[0]), BF16),
            pltpu.VMEM((width, len(LEFT) * BLOCK), BF16),
            pltpu.VMEM((len(RIGHT) * BLOCK, width), BF16),
            pltpu.SemaphoreType.DMA((width // BLOCK,)),
        ],
        compiler_params=pltpu.CompilerParams(vmem_limit_bytes=40 * 2**20),
        name="whiten",
    )(arrived)


def shards(captured, expert_ids):
    device_count = lax.axis_size("tok") * lax.axis_size("exp")
    width = captured.shape[2]
    outbox = route(captured, expert_ids, device_count).reshape(device_count, -1, width)
    arrived = lax.all_to_all(outbox, ("tok", "exp"), split_axis=0, concat_axis=0, tiled=True)
    return whiten(arrived.reshape(-1, width))[None]


def solution(mesh):
    placed = (P(("tok", "exp"), None, None), P(("tok", "exp"), None))
    return jax.shard_map(
        shards, mesh=mesh, in_specs=placed, out_specs=P(("tok", "exp"), None, None), check_vma=False
    )
```

```python
import jax
import jax.numpy as jnp
from jax import lax
from jax.experimental import pallas as pl
from jax.experimental.pallas import tpu as pltpu
from jax.sharding import PartitionSpec as P

damping = 0.1
EMPTY = 32.0
BLOCK = 128
PANEL = 8
F32 = jnp.float32
BF16 = jnp.bfloat16


def iota(shape, dim):
    return lax.broadcasted_iota(jnp.int32, shape, dim)


def route_kernel(device_count, ids_ref, rows_hbm, out_ref, rows_ref, sem):
    fetch = pltpu.make_async_copy(rows_hbm, rows_ref, sem)
    fetch.start()
    top, tokens = ids_ref.shape
    entries = tokens * top
    half = entries // 2
    slots = out_ref.shape[0]
    per_pair = slots // device_count
    ids = ids_ref[...].astype(F32).astype(BF16)
    pick_col = (iota((entries, tokens), 0) // top == iota((entries, tokens), 1)).astype(F32).astype(BF16)
    by_col = lax.dot_general(pick_col, ids, (((1,), (1,)), ((), ())), preferred_element_type=F32)
    keep = iota((entries, top), 0) % top == iota((entries, top), 1)
    id_col = jnp.sum(jnp.where(keep, by_col, 0.0), axis=1, keepdims=True)
    pick_row = (iota((tokens, entries), 1) // top == iota((tokens, entries), 0)).astype(F32).astype(BF16)
    by_row = jnp.dot(ids, pick_row, preferred_element_type=F32)
    keep = iota((top, entries), 1) % top == iota((top, entries), 0)
    id_row = jnp.sum(jnp.where(keep, by_row, 0.0), axis=0, keepdims=True)
    earlier = iota((half, half), 0) < iota((half, half), 1)
    places = []
    for part in range(2):
        col = id_col[part * half : (part + 1) * half]
        row = id_row[:, part * half : (part + 1) * half]
        rank = jnp.sum(jnp.where((col == row) & earlier, 1.0, 0.0), axis=0, keepdims=True)
        places.append(row * per_pair + rank + part * (per_pair // 2))
    place = jnp.concatenate(places, axis=1).astype(jnp.int32)
    fetch.wait()
    tile = 2 * BLOCK
    for first in range(0, slots, tile):
        onehot = jnp.where(iota((tile, entries), 0) + first == place, 1.0, 0.0)
        used = jnp.sum(onehot, axis=1, keepdims=True)
        moved = jnp.dot(onehot.astype(BF16), rows_ref[...], preferred_element_type=F32)
        mark = jnp.where(iota((tile, BLOCK), 1) == 0, EMPTY * (1.0 - used), 0.0)
        out_ref[first : first + tile, :BLOCK] = (moved[:, :BLOCK] + mark).astype(BF16)
        out_ref[first : first + tile, BLOCK:] = moved[:, BLOCK:].astype(BF16)


def route(captured, expert_ids, device_count):
    token_rows, top, width = captured.shape
    slots = token_rows * top * 2
    return pl.pallas_call(
        lambda *refs: route_kernel(device_count, *refs),
        out_shape=jax.ShapeDtypeStruct((slots, width), BF16),
        in_specs=[pl.BlockSpec(memory_space=pltpu.VMEM), pl.BlockSpec(memory_space=pltpu.HBM)],
        out_specs=pl.BlockSpec(memory_space=pltpu.VMEM),
        scratch_shapes=[pltpu.VMEM((token_rows * top, width), BF16), pltpu.SemaphoreType.DMA(())],
        compiler_params=pltpu.CompilerParams(vmem_limit_bytes=32 * 2**20),
        name="route",
    )(expert_ids.T, captured.reshape(token_rows * top, width))


LEFT = (0, 0, 1, 1, 0, 2)
RIGHT = (0, 1, 0, 1, 2, 0)


def pieces(x):
    first = x.astype(BF16)
    rest = x - first.astype(F32)
    second = rest.astype(BF16)
    third = (rest - second.astype(F32)).astype(BF16)
    return first, second, third


def left_stack(x):
    part = pieces(x)
    return jnp.concatenate([part[i] for i in LEFT], axis=1)


def right_stack(x, axis):
    part = pieces(x)
    return jnp.concatenate([part[i] for i in RIGHT], axis=axis)


def along_lanes(x, lane):
    return jnp.take_along_axis(x, jnp.full(x.shape, lane, jnp.int32), axis=1, mode="promise_in_bounds")


def along_sublanes(x, row):
    return jnp.broadcast_to(x[row : row + 1, :], x.shape)


def add_up(terms):
    while len(terms) > 1:
        terms = [a + b for a, b in zip(terms[::2], terms[1::2])]
    return terms[0]


def invert_factor(rows, beside=lambda p: None):
    lane = iota((PANEL, BLOCK), 1)
    sub = iota((PANEL, BLOCK), 0)
    count = len(rows)
    each = range(PANEL)
    for p in range(count):
        base = p * PANEL
        corner = [along_lanes(rows[p], base + j) for j in each]
        below = {}

        def spread(i, base=base, below=below):
            below[i] = [along_lanes(rows[i], base + j) for j in each]

        far = list(range(p + 1, count))
        while far[:1] and far[0] <= p + 2:
            spread(far.pop(0))
        inside = (lane >= base) & (lane < base + PANEL)
        full = jnp.where(inside, jnp.where(lane == sub + base, 1.0, 0.0), rows[p])
        result = full
        if p + 1 < count:
            ahead = list(below[p + 1])
            rows[p + 1] = jnp.where(inside, 0.0, rows[p + 1])
        for j in range(0, PANEL, 2):
            for _ in range(-(-len(far) // ((PANEL - j) // 2))):
                spread(far.pop(0))
            one, two = sub == j, sub == j + 1
            both = one | two
            a, b, c = (along_sublanes(corner[q], r) for q, r in ((j, j), (j + 1, j), (j + 1, j + 1)))
            det = a * c - b * b
            over = 1.0 / det
            left = jnp.where(one, -1.0, jnp.where(two, 0.0, corner[j]))
            right = jnp.where(two, -1.0, jnp.where(one, 0.0, corner[j + 1]))
            left, right = left * c - right * b, right * a - left * b
            left_over, right_over = left * over, right * over

            def sweep(x, soon):
                u, v = along_sublanes(x, j), along_sublanes(x, j + 1)
                kept = jnp.where(both, 0.0, x)
                if soon:
                    return kept - (left * u + right * v) * over
                return kept - (left_over * u + right_over * v)

            u, v = along_sublanes(full, j), along_sublanes(full, j + 1)
            if p + 1 < count:
                one_next = ahead[j] * c - ahead[j + 1] * b
                two_next = ahead[j + 1] * a - ahead[j] * b
                for q in range(j + 2, PANEL):
                    term = one_next * along_sublanes(corner[q], j) + two_next * along_sublanes(corner[q], j + 1)
                    ahead[q] = ahead[q] - term * over
                rows[p + 1] = rows[p + 1] - (one_next * u + two_next * v) * over
            for q in range(j + 2, PANEL):
                corner[q] = sweep(corner[q], q <= j + 3)
            second = (a * v - b * u) * lax.rsqrt(a * det)
            result = jnp.where(one, u * lax.rsqrt(a), jnp.where(two, second, result))
            full = sweep(full, j + 2 == PANEL)
        rows[p] = result
        steps = [along_sublanes(full, j) for j in each]
        for i in range(p + 2, count):
            rows[i] = jnp.where(inside, 0.0, rows[i]) - add_up([below[i][j] * steps[j] for j in each])
        beside(p)


def whiten_kernel(x_ref, out_ref, t_ref, turned_ref, left_ref, right_ref, sems):
    total, width = x_ref.shape
    blocks = width // BLOCK
    panels = BLOCK // PANEL
    contract_lanes = (((1,), (1,)), ((), ()))

    def at(k, stop=None):
        return slice(k * BLOCK, (k + 1 if stop is None else stop) * BLOCK)

    first = iota((BLOCK, BLOCK), 1) == 0

    def squares(i, sums):
        filled, corner, trace = sums
        mine = pl.ds(pl.multiple_of(i * BLOCK, BLOCK), BLOCK)
        head = x_ref[mine, :BLOCK].astype(F32)
        real = first & (head != EMPTY)
        square = jnp.where(real, head * head, 0.0)
        filled = filled + jnp.where(real, 1.0, 0.0)
        corner = corner + square
        trace = trace + jnp.where(first, 0.0, head * head) + square
        for k in range(1, blocks):
            more = x_ref[mine, at(k)].astype(F32)
            trace = trace + more * more
        return filled, corner, trace

    sums = lax.fori_loop(0, total // BLOCK, squares, (jnp.zeros((BLOCK, BLOCK), F32),) * 3)
    rows_here, square, trace = (jnp.sum(part) for part in sums)

    eye = iota((BLOCK, BLOCK), 0) == iota((BLOCK, BLOCK), 1)
    lower = iota((BLOCK, BLOCK), 0) >= iota((BLOCK, BLOCK), 1)
    mean = trace / width
    unit = 1.0 / mean
    scale = jnp.sqrt(rows_here / mean)

    def turn(i):
        turned_ref[at(i), :] = x_ref[:, at(i)].T

    turn(0)
    spd = jnp.dot(turned_ref[at(0), :], x_ref[:, at(0)], preferred_element_type=F32)
    origin = eye & (iota((BLOCK, BLOCK), 0) == 0)
    spd = jnp.where(origin, square, spd) * unit + jnp.where(eye, damping, 0.0)

    def gram(i, n):
        mine, columns = at(i, i + 2), at(n, n + 2)
        block = jnp.dot(turned_ref[mine, :], x_ref[:, columns], preferred_element_type=F32) * unit
        if i == n:
            block = block + jnp.where(iota(block.shape, 0) == iota(block.shape, 1), damping, 0.0)
        t_ref[mine, columns] = block

    pending = [lambda i=i: turn(i) for i in range(1, blocks)]
    pending += [lambda i=i, n=n: gram(i, n) for i in range(0, blocks, 2) for n in range(0, blocks, 2)]
    sends = []

    def beside(p):
        for _ in range(-(-len(pending) // (panels - p))):
            pending.pop(0)()

    for k in range(blocks):
        rows = [spd[p * PANEL : (p + 1) * PANEL] for p in range(panels)]
        invert_factor(rows, beside)
        inverse = jnp.where(lower, jnp.concatenate(rows, axis=0), 0.0)
        inverse_left = left_stack(inverse)
        inverse_right = right_stack(inverse, 1)
        if k + 1 < blocks:
            across = jnp.dot(
                inverse_left, right_stack(t_ref[at(k), at(k + 1)], 0), preferred_element_type=F32
            )
            down = lax.dot_general(
                left_stack(t_ref[at(k + 1), at(k)]), inverse_right, contract_lanes, preferred_element_type=F32
            )
            spd = t_ref[at(k + 1), at(k + 1)] - jnp.dot(left_stack(down), right_stack(across, 0), preferred_element_type=F32)

        def solve(n, k=k, inverse=inverse, inverse_left=inverse_left):
            for m in (n, n + 1):
                if m == k:
                    right_ref[:, at(m)] = right_stack(inverse, 0)
                    t_ref[at(k), at(m)] = inverse * scale
            if n != k and n + 1 != k:
                parts = [(n, 2)]
            else:
                parts = [(n + 1 if n == k else n, 1)]
            for m, size in parts:
                columns = at(m, m + size)
                solved = jnp.dot(inverse_left, right_stack(t_ref[at(k), columns], 0), preferred_element_type=F32)
                right_ref[:, columns] = right_stack(solved, 0)
                t_ref[at(k), columns] = solved * scale if m < k else jnp.zeros_like(solved)

        def descend(i, k=k, inverse_right=inverse_right):
            left_ref[at(i), :] = left_stack(
                lax.dot_general(
                    left_stack(t_ref[at(i), at(k)]), inverse_right, contract_lanes, preferred_element_type=F32
                )
            )
            t_ref[at(i), at(k)] = jnp.zeros((BLOCK, BLOCK), F32)

        def update(i, n, k=k):
            columns = at(n, n + 2)
            t_ref[at(i), columns] -= jnp.dot(left_ref[at(i), :], right_ref[:, columns], preferred_element_type=F32)

        def send(k=k):
            sends.append(pltpu.make_async_copy(t_ref.at[at(k), :], out_ref.at[at(k), :], sems.at[k]))
            sends[-1].start()

        pending = [lambda n=n, solve=solve: solve(n) for n in range(0, blocks, 2)]
        pending += [send]
        pending += [lambda i=i, descend=descend: descend(i) for i in range(k + 1, blocks)]
        pending += [
            lambda i=i, n=n, update=update: update(i, n)
            for n in range(0, blocks, 2)
            for i in range(k + 1, blocks)
        ]
    while pending:
        pending.pop(0)()
    for copy in sends:
        copy.wait()


def whiten(arrived):
    width = arrived.shape[1]
    return pl.pallas_call(
        whiten_kernel,
        out_shape=jax.ShapeDtypeStruct((width, width), F32),
        in_specs=[pl.BlockSpec(memory_space=pltpu.VMEM)],
        out_specs=pl.BlockSpec(memory_space=pltpu.HBM),
        scratch_shapes=[
            pltpu.VMEM((width, width), F32),
            pltpu.VMEM((width, arrived.shape[0]), BF16),
            pltpu.VMEM((width, len(LEFT) * BLOCK), BF16),
            pltpu.VMEM((len(RIGHT) * BLOCK, width), BF16),
            pltpu.SemaphoreType.DMA((width // BLOCK,)),
        ],
        compiler_params=pltpu.CompilerParams(vmem_limit_bytes=40 * 2**20),
        name="whiten",
    )(arrived)


def shards(captured, expert_ids):
    device_count = lax.axis_size("tok") * lax.axis_size("exp")
    width = captured.shape[2]
    outbox = route(captured, expert_ids, device_count).reshape(device_count, -1, width)
    arrived = lax.all_to_all(outbox, ("tok", "exp"), split_axis=0, concat_axis=0, tiled=True)
    return whiten(arrived.reshape(-1, width))[None]


def solution(mesh):
    placed = (P(("tok", "exp"), None, None), P(("tok", "exp"), None))
    return jax.shard_map(
        shards, mesh=mesh, in_specs=placed, out_specs=P(("tok", "exp"), None, None), check_vma=False
    )
```

```python
import jax
import jax.numpy as jnp
from jax import lax
from jax.experimental import pallas as pl
from jax.experimental.pallas import tpu as pltpu
from jax.sharding import PartitionSpec as P

damping = 0.1
EMPTY = 32.0
BLOCK = 128
PANEL = 8
F32 = jnp.float32
BF16 = jnp.bfloat16


def iota(shape, dim):
    return lax.broadcasted_iota(jnp.int32, shape, dim)


def route_kernel(device_count, ids_ref, rows_hbm, out_ref, rows_ref, sem):
    fetch = pltpu.make_async_copy(rows_hbm, rows_ref, sem)
    fetch.start()
    top, tokens = ids_ref.shape
    entries = tokens * top
    half = entries // 2
    slots = out_ref.shape[0]
    per_pair = slots // device_count
    ids = ids_ref[...].astype(F32).astype(BF16)
    pick_col = (iota((entries, tokens), 0) // top == iota((entries, tokens), 1)).astype(F32).astype(BF16)
    by_col = lax.dot_general(pick_col, ids, (((1,), (1,)), ((), ())), preferred_element_type=F32)
    keep = iota((entries, top), 0) % top == iota((entries, top), 1)
    id_col = jnp.sum(jnp.where(keep, by_col, 0.0), axis=1, keepdims=True)
    pick_row = (iota((tokens, entries), 1) // top == iota((tokens, entries), 0)).astype(F32).astype(BF16)
    by_row = jnp.dot(ids, pick_row, preferred_element_type=F32)
    keep = iota((top, entries), 1) % top == iota((top, entries), 0)
    id_row = jnp.sum(jnp.where(keep, by_row, 0.0), axis=0, keepdims=True)
    earlier = iota((half, half), 0) < iota((half, half), 1)
    places = []
    for part in range(2):
        col = id_col[part * half : (part + 1) * half]
        row = id_row[:, part * half : (part + 1) * half]
        rank = jnp.sum(jnp.where((col == row) & earlier, 1.0, 0.0), axis=0, keepdims=True)
        places.append(row * per_pair + rank + part * (per_pair // 2))
    place = jnp.concatenate(places, axis=1).astype(jnp.int32)
    fetch.wait()
    tile = 2 * BLOCK
    for first in range(0, slots, tile):
        onehot = jnp.where(iota((tile, entries), 0) + first == place, 1.0, 0.0)
        used = jnp.sum(onehot, axis=1, keepdims=True)
        moved = jnp.dot(onehot.astype(BF16), rows_ref[...], preferred_element_type=F32)
        mark = jnp.where(iota((tile, BLOCK), 1) == 0, EMPTY * (1.0 - used), 0.0)
        out_ref[first : first + tile, :BLOCK] = (moved[:, :BLOCK] + mark).astype(BF16)
        out_ref[first : first + tile, BLOCK:] = moved[:, BLOCK:].astype(BF16)


def route(captured, expert_ids, device_count):
    token_rows, top, width = captured.shape
    slots = token_rows * top * 2
    return pl.pallas_call(
        lambda *refs: route_kernel(device_count, *refs),
        out_shape=jax.ShapeDtypeStruct((slots, width), BF16),
        in_specs=[pl.BlockSpec(memory_space=pltpu.VMEM), pl.BlockSpec(memory_space=pltpu.HBM)],
        out_specs=pl.BlockSpec(memory_space=pltpu.VMEM),
        scratch_shapes=[pltpu.VMEM((token_rows * top, width), BF16), pltpu.SemaphoreType.DMA(())],
        compiler_params=pltpu.CompilerParams(vmem_limit_bytes=32 * 2**20),
        name="route",
    )(expert_ids.T, captured.reshape(token_rows * top, width))


LEFT = (0, 0, 1, 1, 0, 2)
RIGHT = (0, 1, 0, 1, 2, 0)


def pieces(x):
    first = x.astype(BF16)
    rest = x - first.astype(F32)
    second = rest.astype(BF16)
    third = (rest - second.astype(F32)).astype(BF16)
    return first, second, third


def left_stack(x):
    part = pieces(x)
    return jnp.concatenate([part[i] for i in LEFT], axis=1)


def right_stack(x, axis):
    part = pieces(x)
    return jnp.concatenate([part[i] for i in RIGHT], axis=axis)


def along_lanes(x, lane):
    return jnp.take_along_axis(x, jnp.full(x.shape, lane, jnp.int32), axis=1, mode="promise_in_bounds")


def along_sublanes(x, row):
    return jnp.broadcast_to(x[row : row + 1, :], x.shape)


def add_up(terms):
    while len(terms) > 1:
        terms = [a + b for a, b in zip(terms[::2], terms[1::2])]
    return terms[0]


def invert_factor(rows, beside=lambda p: None):
    lane = iota((PANEL, BLOCK), 1)
    sub = iota((PANEL, BLOCK), 0)
    count = len(rows)
    each = range(PANEL)
    for p in range(count):
        base = p * PANEL
        corner = [along_lanes(rows[p], base + j) for j in each]
        below = {}

        def spread(i, base=base, below=below):
            below[i] = [along_lanes(rows[i], base + j) for j in each]

        far = list(range(p + 1, count))
        while far[:1] and far[0] <= p + 2:
            spread(far.pop(0))
        inside = (lane >= base) & (lane < base + PANEL)
        full = jnp.where(inside, jnp.where(lane == sub + base, 1.0, 0.0), rows[p])
        result = full
        if p + 1 < count:
            ahead = list(below[p + 1])
            rows[p + 1] = jnp.where(inside, 0.0, rows[p + 1])
        for j in range(0, PANEL, 2):
            for _ in range(-(-len(far) // ((PANEL - j) // 2))):
                spread(far.pop(0))
            one, two = sub == j, sub == j + 1
            both = one | two
            a, b, c = (along_sublanes(corner[q], r) for q, r in ((j, j), (j + 1, j), (j + 1, j + 1)))
            det = a * c - b * b
            over = 1.0 / det
            left = jnp.where(one, -1.0, jnp.where(two, 0.0, corner[j]))
            right = jnp.where(two, -1.0, jnp.where(one, 0.0, corner[j + 1]))
            left, right = left * c - right * b, right * a - left * b
            left_over, right_over = left * over, right * over

            def sweep(x, soon):
                u, v = along_sublanes(x, j), along_sublanes(x, j + 1)
                kept = jnp.where(both, 0.0, x)
                if soon:
                    return kept - (left * u + right * v) * over
                return kept - (left_over * u + right_over * v)

            u, v = along_sublanes(full, j), along_sublanes(full, j + 1)
            if p + 1 < count:
                one_next = ahead[j] * c - ahead[j + 1] * b
                two_next = ahead[j + 1] * a - ahead[j] * b
                for q in range(j + 2, PANEL):
                    term = one_next * along_sublanes(corner[q], j) + two_next * along_sublanes(corner[q], j + 1)
                    ahead[q] = ahead[q] - term * over
                rows[p + 1] = rows[p + 1] - (one_next * u + two_next * v) * over
            for q in range(j + 2, PANEL):
                corner[q] = sweep(corner[q], q <= j + 3)
            second = (a * v - b * u) * lax.rsqrt(a * det)
            result = jnp.where(one, u * lax.rsqrt(a), jnp.where(two, second, result))
            full = sweep(full, j + 2 == PANEL)
        rows[p] = result
        steps = [along_sublanes(full, j) for j in each]
        for i in range(p + 2, count):
            rows[i] = jnp.where(inside, 0.0, rows[i]) - add_up([below[i][j] * steps[j] for j in each])
        beside(p)


def whiten_kernel(x_ref, out_ref, t_ref, turned_ref, left_ref, right_ref, sems):
    total, width = x_ref.shape
    blocks = width // BLOCK
    panels = BLOCK // PANEL
    contract_lanes = (((1,), (1,)), ((), ()))

    def at(k, stop=None):
        return slice(k * BLOCK, (k + 1 if stop is None else stop) * BLOCK)

    first = iota((BLOCK, BLOCK), 1) == 0

    def squares(i, sums):
        filled, corner, trace = sums
        mine = pl.ds(pl.multiple_of(i * BLOCK, BLOCK), BLOCK)
        head = x_ref[mine, :BLOCK].astype(F32)
        real = first & (head != EMPTY)
        square = jnp.where(real, head * head, 0.0)
        filled = filled + jnp.where(real, 1.0, 0.0)
        corner = corner + square
        trace = trace + jnp.where(first, 0.0, head * head) + square
        for k in range(1, blocks):
            more = x_ref[mine, at(k)].astype(F32)
            trace = trace + more * more
        return filled, corner, trace

    sums = lax.fori_loop(0, total // BLOCK, squares, (jnp.zeros((BLOCK, BLOCK), F32),) * 3)
    rows_here, square, trace = (jnp.sum(part) for part in sums)

    eye = iota((BLOCK, BLOCK), 0) == iota((BLOCK, BLOCK), 1)
    lower = iota((BLOCK, BLOCK), 0) >= iota((BLOCK, BLOCK), 1)
    mean = trace / width
    unit = 1.0 / mean
    scale = jnp.sqrt(rows_here / mean)

    def turn(i):
        turned_ref[at(i), :] = x_ref[:, at(i)].T

    turn(0)
    spd = jnp.dot(turned_ref[at(0), :], x_ref[:, at(0)], preferred_element_type=F32)
    origin = eye & (iota((BLOCK, BLOCK), 0) == 0)
    spd = jnp.where(origin, square, spd) * unit + jnp.where(eye, damping, 0.0)

    def gram(i, n):
        mine, columns = at(i, i + 2), at(n, n + 2)
        block = jnp.dot(turned_ref[mine, :], x_ref[:, columns], preferred_element_type=F32) * unit
        if i == n:
            block = block + jnp.where(iota(block.shape, 0) == iota(block.shape, 1), damping, 0.0)
        t_ref[mine, columns] = block

    pending = [lambda i=i: turn(i) for i in range(1, blocks)]
    pending += [lambda i=i, n=n: gram(i, n) for i in range(0, blocks, 2) for n in range(0, blocks, 2)]
    sends = []

    def beside(p):
        for _ in range(-(-len(pending) // (panels - p))):
            pending.pop(0)()

    for k in range(blocks):
        rows = [spd[p * PANEL : (p + 1) * PANEL] for p in range(panels)]
        invert_factor(rows, beside)
        inverse = jnp.where(lower, jnp.concatenate(rows, axis=0), 0.0)
        inverse_left = left_stack(inverse)
        inverse_right = right_stack(inverse, 1)
        if k + 1 < blocks:
            across = jnp.dot(
                inverse_left, right_stack(t_ref[at(k), at(k + 1)], 0), preferred_element_type=F32
            )
            down = lax.dot_general(
                left_stack(t_ref[at(k + 1), at(k)]), inverse_right, contract_lanes, preferred_element_type=F32
            )
            left_ref[at(k + 1), :] = left_stack(down)
            t_ref[at(k + 1), at(k)] = jnp.zeros((BLOCK, BLOCK), F32)
            spd = t_ref[at(k + 1), at(k + 1)] - jnp.dot(left_stack(down), right_stack(across, 0), preferred_element_type=F32)

        def solve(n, k=k, inverse=inverse, inverse_left=inverse_left):
            for m in (n, n + 1):
                if m == k:
                    right_ref[:, at(m)] = right_stack(inverse, 0)
                    t_ref[at(k), at(m)] = inverse * scale
            if n != k and n + 1 != k:
                parts = [(n, 2)]
            else:
                parts = [(n + 1 if n == k else n, 1)]
            for m, size in parts:
                columns = at(m, m + size)
                solved = jnp.dot(inverse_left, right_stack(t_ref[at(k), columns], 0), preferred_element_type=F32)
                right_ref[:, columns] = right_stack(solved, 0)
                t_ref[at(k), columns] = solved * scale if m < k else jnp.zeros_like(solved)

        def descend(i, k=k, inverse_right=inverse_right):
            left_ref[at(i), :] = left_stack(
                lax.dot_general(
                    left_stack(t_ref[at(i), at(k)]), inverse_right, contract_lanes, preferred_element_type=F32
                )
            )
            t_ref[at(i), at(k)] = jnp.zeros((BLOCK, BLOCK), F32)

        def update(i, n, k=k):
            columns = at(n, n + 2)
            t_ref[at(i), columns] -= jnp.dot(left_ref[at(i), :], right_ref[:, columns], preferred_element_type=F32)

        def send(k=k):
            sends.append(pltpu.make_async_copy(t_ref.at[at(k), :], out_ref.at[at(k), :], sems.at[k]))
            sends[-1].start()

        pending = [lambda n=n, solve=solve: solve(n) for n in range(0, blocks, 2)]
        pending += [send]
        pending += [lambda i=i, descend=descend: descend(i) for i in range(k + 2, blocks)]
        pending += [
            lambda i=i, n=n, update=update: update(i, n)
            for n in range(0, blocks, 2)
            for i in range(k + 1, blocks)
        ]
    while pending:
        pending.pop(0)()
    for copy in sends:
        copy.wait()


def whiten(arrived):
    width = arrived.shape[1]
    return pl.pallas_call(
        whiten_kernel,
        out_shape=jax.ShapeDtypeStruct((width, width), F32),
        in_specs=[pl.BlockSpec(memory_space=pltpu.VMEM)],
        out_specs=pl.BlockSpec(memory_space=pltpu.HBM),
        scratch_shapes=[
            pltpu.VMEM((width, width), F32),
            pltpu.VMEM((width, arrived.shape[0]), BF16),
            pltpu.VMEM((width, len(LEFT) * BLOCK), BF16),
            pltpu.VMEM((len(RIGHT) * BLOCK, width), BF16),
            pltpu.SemaphoreType.DMA((width // BLOCK,)),
        ],
        compiler_params=pltpu.CompilerParams(vmem_limit_bytes=40 * 2**20),
        name="whiten",
    )(arrived)


def shards(captured, expert_ids):
    device_count = lax.axis_size("tok") * lax.axis_size("exp")
    width = captured.shape[2]
    outbox = route(captured, expert_ids, device_count).reshape(device_count, -1, width)
    arrived = lax.all_to_all(outbox, ("tok", "exp"), split_axis=0, concat_axis=0, tiled=True)
    return whiten(arrived.reshape(-1, width))[None]


def solution(mesh):
    placed = (P(("tok", "exp"), None, None), P(("tok", "exp"), None))
    return jax.shard_map(
        shards, mesh=mesh, in_specs=placed, out_specs=P(("tok", "exp"), None, None), check_vma=False
    )
```
